128 devices in a mesh: dp: 16 (over x_hi, y, core), tensor: 8 (over x_lo, z).
Axes of the slice: x: 4 (x_hi: 2, x_lo: 2; x = x_hi * 2 + x_lo), y: 4, z: 4, core: 2. Of those that a mesh axis runs over, the one named last changes fastest.
Arguments:
- train_acts: bfloat16 [2048, 5120], P('dp', 'tensor'), may hold values from -6 to 6
- train_grads: bfloat16 [2048, 13824], P('dp', 'tensor'), may hold values from -0.0011672974 to 0.0011672974
- query_acts: bfloat16 [128, 5120], P('dp', 'tensor'), may hold values from -6 to 6
- query_grads: bfloat16 [128, 13824], P('dp', 'tensor'), may hold values from -6 to 6
- in_basis: bfloat16 [5120, 5120], P('dp', 'tensor'), may hold values from -0.078125 to 0.078125
- out_basis: bfloat16 [13824, 13824], P('tensor', 'dp'), may hold values from -0.0546875 to 0.0546875
- eigvals: float32 [13824, 5120], P('dp', 'tensor'), may hold values from 0.02 to 5
- lengths: int32 [16], P('dp'), may hold values from 32 to 128, as said below
Outputs:
- token_scores: float32 [2, 2048], P(None, ('dp', 'tensor'))
- seq_scores: float32 [2, 16], P(None, 'dp')
The draws below stay inside these ranges and needn't reach their ends.
Inputs may be any that keep to these rules, and one draw needn't show every extreme that they name: `lengths`: each sequence's valid tokens come first and the rest is padding.
All inputs are finite; a program needn't handle non-finite values.
Results may differ from the reference program's by a relative error of at most 0.0053.
Values may be sent and summed in bfloat16 or wider, within the bound.
No kernel may reach another device: no remote copies, remote signals or barrier semaphores. Data moves between devices by JAX's collectives and lax.ppermute only.
A program may use at most 128 MiB of HBM per device.

```python
import math
import jax
import jax.numpy as jnp

D = 5120
FF = 13824
SEQLEN = 128
QUERIES = 2
TOKENS = 2048
SEQS = 16
QROWS = 128


def draw_lengths(key, part):
    key = jax.random.fold_in(key, 5)
    key_base, key_top, key_low = jax.random.split(key, 3)
    base = jax.random.randint(key_base, (SEQS,), SEQLEN // 4, SEQLEN + 1)
    top_index = jax.random.randint(key_top, (), 0, SEQS)
    low_index = (top_index + 1 + jax.random.randint(key_low, (), 0, SEQS - 1)) % SEQS
    offsets = jnp.arange(SEQS, dtype=jnp.int32)
    filled = jnp.where(offsets == top_index, SEQLEN, base)
    return jnp.where(offsets == low_index, SEQLEN // 4, filled).astype(jnp.int32)


def steps_of(own_key, dims, cuts, least, high):
    def one(axis_at, blocks):
        draws = jax.random.uniform(jax.random.fold_in(jax.random.fold_in(own_key, 6), axis_at), (blocks,), jnp.float32, least / len(cuts), high / len(cuts))
        return jnp.repeat(jnp.exp(draws), dims[axis_at] // blocks).reshape((-1,) + (1,) * (len(dims) - axis_at - 1))

    factor_of = one(*cuts[0])
    for cut in cuts[1:]:
        factor_of = factor_of * one(*cut)
    return factor_of


def gaussian(key, extent, deviation, reach, shards=(), kind=jnp.bfloat16):
    gain = steps_of(key, extent, shards, -0.22, 0.18) if shards else 1.0
    result = jax.random.normal(key, extent, jnp.float32) * deviation * gain
    return jnp.minimum(jnp.maximum(result, -reach), reach).astype(kind)


def setup_inputs(seed: int = 0) -> dict:
    streams_of = jax.random.split(jax.random.key(seed), 9)
    train_acts = gaussian(streams_of[0], (TOKENS, D), 1.0, 6.0, ((0, 16), (1, 8)))
    train_grads = gaussian(streams_of[1], (TOKENS, FF), (1.0 / D), 0.0011672974, ((0, 16), (1, 8)))
    query_acts = gaussian(streams_of[2], (QROWS, D), 1.0, 6.0, ((0, 16), (1, 8)))
    query_grads = gaussian(streams_of[3], (QROWS, FF), 1.0, 6.0, ((0, 16), (1, 8)))
    in_basis = gaussian(streams_of[4], (D, D), D ** -0.5, 0.078125, ((0, 16), (1, 8)))
    out_basis = gaussian(streams_of[5], (FF, FF), FF ** -0.5, 0.0546875, ((0, 8), (1, 16)))
    eigvals = jnp.clip(jnp.exp(math.log(5.0) - 5.521461 * jax.random.uniform(streams_of[6], (FF, D), jnp.float32) ** steps_of(streams_of[6], (FF, D), ((0, 16), (1, 8)), -0.2, 0.2)), 0.02, 5.0)
    lengths = draw_lengths(jax.random.fold_in(streams_of[8], 71), 0)
    return dict(train_acts=train_acts, train_grads=train_grads, query_acts=query_acts, query_grads=query_grads, in_basis=in_basis, out_basis=out_basis, eigvals=eigvals, lengths=lengths)


damping = 0.1


def reference(train_acts, train_grads, query_acts, query_grads, in_basis, out_basis, eigvals, lengths):
    rot_train_acts = jnp.dot(train_acts, in_basis, preferred_element_type=jnp.float32).astype(jnp.bfloat16)
    rot_query_acts = jnp.dot(query_acts, in_basis, preferred_element_type=jnp.float32).astype(jnp.bfloat16)
    rot_train_grads = jnp.dot(train_grads, out_basis, preferred_element_type=jnp.float32).astype(jnp.bfloat16)
    rot_query_grads = jnp.dot(query_grads, out_basis, preferred_element_type=jnp.float32).astype(jnp.bfloat16)
    query_len = QROWS // QUERIES
    acts_wide = rot_train_acts.astype(jnp.float32)
    results = []
    for query in range(QUERIES):
        grad_part = rot_query_grads[query * query_len:(query + 1) * query_len]
        act_part = rot_query_acts[query * query_len:(query + 1) * query_len]
        numerator = jnp.dot(grad_part.T, act_part, preferred_element_type=jnp.float32)
        precond = (numerator / (query_len * (eigvals + damping))).astype(jnp.bfloat16)
        projected = jnp.dot(rot_train_grads, precond, preferred_element_type=jnp.float32)
        results.append(jnp.sum(projected * acts_wide, axis=1))
    raw = jnp.stack(results, axis=0)
    offsets = jnp.arange(TOKENS, dtype=jnp.int32)
    position = offsets % SEQLEN
    sequence = offsets // SEQLEN
    valid = (position < lengths[sequence]).astype(jnp.float32)
    token_scores = raw * valid[None, :]
    seq_scores = jnp.sum(token_scores.reshape(QUERIES, SEQS, SEQLEN), axis=2)
    return token_scores, seq_scores
```

```python
import jax
import jax.numpy as jnp
from jax import lax
from jax.sharding import PartitionSpec as P

SEQLEN = 128
QUERIES = 2


damping = 0.1


def per_device(
    train_acts, train_grads, query_acts, query_grads, in_basis, out_basis, eigvals, lengths
):
    tok_rows = train_acts.shape[0]
    query_rows = query_acts.shape[0]
    block_rows = tok_rows + query_rows
    n_data = lax.axis_size("dp")
    n_tensor = lax.axis_size("tensor")
    grad_local = jnp.concatenate([train_grads, query_grads], axis=0)
    grad_partial = jnp.dot(
        lax.all_gather(grad_local, "dp", axis=0, tiled=True),
        out_basis,
        preferred_element_type=jnp.float32,
    )
    rotated_grads = lax.psum(grad_partial, "tensor").astype(jnp.bfloat16)
    grouped_grads = rotated_grads.reshape(n_data, block_rows, rotated_grads.shape[1])
    train_rot_grads = grouped_grads[:, :tok_rows].reshape(n_data * tok_rows, -1)
    query_rot_grads = grouped_grads[:, tok_rows:].reshape(n_data * query_rows, -1)
    act_local = jnp.concatenate([train_acts, query_acts], axis=0)
    widened = lax.all_gather(act_local, "tensor", axis=1, tiled=True)
    blocks = lax.all_to_all(widened, "dp", split_axis=1, concat_axis=0, tiled=True)
    act_partial = jnp.dot(blocks, in_basis, preferred_element_type=jnp.float32)
    rotated_acts = lax.psum(act_partial, "dp").astype(jnp.bfloat16)
    grouped_acts = rotated_acts.reshape(n_data, block_rows, rotated_acts.shape[1])
    train_rot_acts = grouped_acts[:, :tok_rows].reshape(n_data * tok_rows, -1)
    query_rot_acts = grouped_acts[:, tok_rows:].reshape(n_data * query_rows, -1)
    query_len = query_rot_grads.shape[0] // QUERIES
    acts_wide = train_rot_acts.astype(jnp.float32)
    divisor = query_len * (eigvals + damping)
    results = []
    for query in range(QUERIES):
        grad_part = query_rot_grads[query * query_len : (query + 1) * query_len]
        act_part = query_rot_acts[query * query_len : (query + 1) * query_len]
        numerator = jnp.dot(grad_part.T, act_part, preferred_element_type=jnp.float32)
        precond = (numerator / divisor).astype(jnp.bfloat16)
        projected = jnp.dot(train_rot_grads, precond, preferred_element_type=jnp.float32)
        results.append(jnp.sum(projected * acts_wide, axis=1))
    partial_scores = jnp.stack(results, axis=0)
    own_count = tok_rows // n_tensor
    by_sequence = partial_scores.reshape(QUERIES, n_data, tok_rows).transpose(1, 0, 2)
    spread = jnp.broadcast_to(by_sequence[:, None], (n_data, n_tensor, QUERIES, tok_rows))
    received = lax.all_to_all(
        spread.reshape(n_data * n_tensor, QUERIES, tok_rows), ("dp", "tensor"), 0, 0, tiled=True
    )
    raw = jnp.sum(received, axis=0)
    valid = (jnp.arange(tok_rows, dtype=jnp.int32) % SEQLEN < lengths[0]).astype(jnp.float32)
    scores = raw * valid[None, :]
    seq_scores = jnp.sum(scores, axis=1, keepdims=True)
    token_scores = lax.dynamic_slice_in_dim(
        scores, lax.axis_index("tensor") * own_count, own_count, axis=1
    )
    return (token_scores, seq_scores)


def solution(mesh):
    placed = (
        P("dp", "tensor"),
        P("dp", "tensor"),
        P("dp", "tensor"),
        P("dp", "tensor"),
        P("dp", "tensor"),
        P("tensor", "dp"),
        P("dp", "tensor"),
        P("dp"),
    )
    return jax.shard_map(
        per_device,
        mesh=mesh,
        in_specs=placed,
        out_specs=(P(None, ("dp", "tensor")), P(None, "dp")),
        check_vma=False,
    )
```

```python
import jax
import jax.numpy as jnp
from jax import lax
from jax.experimental import pallas as pl
from jax.experimental.pallas import tpu as pltpu
from jax.sharding import PartitionSpec as P

SEQLEN = 128
QUERIES = 2
AXES = ("x_hi", "y", "core", "x_lo", "z")
CHIPS = ("x_hi", "y")
TENSOR = ("x_lo", "z")
SIZES = (2, 4, 2, 2, 4)
ROWS = 16
LANES = 128
GROUP = 4
VMEM_BYTES = 24 * 1024 * 1024
VMEM = pl.BlockSpec(memory_space=pltpu.VMEM)
SMEM = pl.BlockSpec(memory_space=pltpu.SMEM)
PARAMS = pltpu.CompilerParams(vmem_limit_bytes=VMEM_BYTES)


damping = 0.1


def take(x, axis, step):
    count = lax.axis_size(axis)
    return lax.ppermute(x, axis, [(i, (i - step) % count) for i in range(count)])


def after(x, *earlier):
    return lax.optimization_barrier((x,) + earlier)[0]


def turn(blocks, axis, shift):
    count = blocks.shape[axis]
    return lax.dynamic_slice_in_dim(
        jnp.concatenate([blocks, blocks], axis=axis), shift, count, axis=axis
    )


def pick_kernel(order, blocks, out):
    for i in range(out.shape[0]):
        out[i] = blocks[order[i]]


def pick(order, blocks):
    return pl.pallas_call(
        pick_kernel,
        out_shape=jax.ShapeDtypeStruct(blocks.shape, blocks.dtype),
        in_specs=[SMEM, VMEM],
        out_specs=VMEM,
        compiler_params=PARAMS,
        name="pick",
    )(order, blocks)


def own_rows_first(rows, x_lo, z):
    order = jnp.stack([(x_lo ^ dx) * 4 + (z + dz) % 4 for dz in range(4) for dx in range(2)])
    return pick(order.astype(jnp.int32), rows.reshape(8, ROWS, -1)).reshape(rows.shape)


def both_cores(x):
    x = x.astype(jnp.float32)
    other = take(x, "core", 1)
    one, two = lax.optimization_barrier(
        (jnp.concatenate([x, other], axis=0), jnp.concatenate([other, x], axis=0))
    )
    return one.astype(jnp.bfloat16), two.astype(jnp.bfloat16)


def rotate_kernel(g0, g1, g2, g3, own_basis, sib_basis, near, up, down, far_own, far_sib, query):
    rows = jnp.concatenate([g0[...], g1[...], g2[...], g3[...]], axis=0)
    shard = g0.shape[0]
    for block, basis in enumerate((own_basis, sib_basis)):
        product = jnp.dot(rows, basis[...], preferred_element_type=jnp.float32)
        for dz in range(4):
            for dx in range(2):
                for s in range(GROUP):
                    start = s * shard + (dz * 2 + dx) * ROWS
                    piece = product[start : start + ROWS]
                    at = (dx * GROUP + s) * ROWS
                    if dz == 2:
                        target = (far_own, far_sib)[block]
                        target[at : at + ROWS, :] = piece
                    else:
                        target = (near, up, None, down)[dz]
                        target[block, at : at + ROWS, :] = piece
        if block == 0:
            for s in range(GROUP):
                start = s * shard + SEQLEN
                query[s] = product[start : start + ROWS]


def rotate(shards, own_basis, sib_basis):
    width = own_basis.shape[1]
    pair = jax.ShapeDtypeStruct((2, 2 * GROUP * ROWS, width), jnp.float32)
    single = jax.ShapeDtypeStruct((2 * GROUP * ROWS, width), jnp.float32)
    query = jax.ShapeDtypeStruct((GROUP, ROWS, width), jnp.float32)
    return pl.pallas_call(
        rotate_kernel,
        out_shape=(pair, pair, pair, single, single, query),
        in_specs=[VMEM] * 6,
        out_specs=(VMEM,) * 6,
        compiler_params=PARAMS,
        cost_estimate=pl.CostEstimate(
            flops=2 * 576 * 1728 * 1728, bytes_accessed=12 * 1024 * 1024, transcendentals=0
        ),
        name="rotate",
    )(*shards, own_basis, sib_basis)


def sum_z_kernel(near, up, down, kept, other):
    half = GROUP * ROWS
    for block in range(2):
        total = near[block] + up[block] + down[block]
        kept[block] = total[:half]
        other[block] = total[half:]


def sum_z(*arrays):
    width = arrays[0].shape[2]
    part = jax.ShapeDtypeStruct((2, GROUP * ROWS, width), jnp.float32)
    return pl.pallas_call(
        sum_z_kernel,
        out_shape=(part, part),
        in_specs=[VMEM] * 3,
        out_specs=(VMEM, VMEM),
        compiler_params=PARAMS,
        cost_estimate=pl.CostEstimate(
            flops=4 * 64 * 864, bytes_accessed=2 * 1024 * 1024, transcendentals=0
        ),
        name="sum_z",
    )(*arrays)


def score_kernel(*refs):
    near, far, acts, (own_precond, sib_precond, out) = refs[:4], refs[4], refs[5:9], refs[9:]
    own = jnp.concatenate([b[0] for b in near] + [far[i, 0] for i in range(4)], axis=0)
    sib = jnp.concatenate([b[1] for b in near] + [far[i, 1] for i in range(4)], axis=0)
    acts = [x[...].astype(jnp.float32) for x in acts]
    wide = []
    for dx in range(2):
        for dz in range(4):
            start = (dz * 2 + dx) * ROWS
            wide += [x[start : start + ROWS] for x in acts]
    wide = jnp.concatenate(wide, axis=0)
    for k in range(QUERIES):
        projected = jnp.dot(own, own_precond[k], preferred_element_type=jnp.float32)
        projected += jnp.dot(sib, sib_precond[k], preferred_element_type=jnp.float32)
        out[:, k : k + 1] = jnp.sum(projected * wide, axis=1, keepdims=True)


def score(blocks, acts, own_precond, sib_precond):
    out = pl.pallas_call(
        score_kernel,
        out_shape=jax.ShapeDtypeStruct((GROUP * SEQLEN, QUERIES), jnp.float32),
        in_specs=[VMEM] * 11,
        out_specs=VMEM,
        compiler_params=PARAMS,
        cost_estimate=pl.CostEstimate(
            flops=2 * 512 * 1728 * 1280, bytes_accessed=8 * 1024 * 1024, transcendentals=0
        ),
        name="score",
    )(*blocks, *acts, own_precond, sib_precond)
    return out.reshape(2, 4, GROUP, ROWS, QUERIES)


def act_kernel(order, acts, *refs):
    bases, (kept, other) = refs[:8], refs[8:]
    total = jnp.zeros((acts.shape[1], kept.shape[1]), jnp.float32)
    for m in range(8):
        total += jnp.dot(acts[order[m]], bases[m][...], preferred_element_type=jnp.float32)
    half = acts.shape[1] // 2
    kept[...] = total[:half]
    other[...] = total[half:]


def rotate_acts(order, acts, bases):
    part = jax.ShapeDtypeStruct((acts.shape[1] // 2, bases[0].shape[1]), jnp.float32)
    return pl.pallas_call(
        act_kernel,
        out_shape=(part, part),
        in_specs=[SMEM] + [VMEM] * 9,
        out_specs=(VMEM, VMEM),
        compiler_params=PARAMS,
        cost_estimate=pl.CostEstimate(
            flops=2 * 288 * 2560 * 640, bytes_accessed=6 * 1024 * 1024, transcendentals=0
        ),
        name="rotate_acts",
    )(order, acts, *bases)


def gather_chips(x, hold=None):
    held = {(0, 0): x, (1, 0): take(x, "x_hi", 1)}
    held[0, 1] = take(x, "y", 1)
    held[0, 3] = take(x, "y", -1)
    partner = held[1, 0] if hold is None else after(held[1, 0], hold)
    held[1, 1] = take(partner, "y", 1)
    held[1, 3] = take(partner, "y", -1)
    held[0, 2] = take(held[0, 1], "y", 1)
    held[1, 2] = take(held[1, 3], "y", -1)
    return held


def pad_to(x, *shape, value=0):
    return jnp.pad(x, [(0, n - m) for m, n in zip(x.shape, shape)], constant_values=value)


def per_device(
    train_acts, train_grads, query_acts, query_grads, in_basis, out_basis, eigvals, lengths
):
    x_hi = lax.axis_index("x_hi")
    y = lax.axis_index("y")
    core = lax.axis_index("core")
    x_lo = lax.axis_index("x_lo")
    z = lax.axis_index("z")

    rows_in, rows_out = out_basis.shape
    deep = -(-rows_in // LANES) * LANES
    wide = -(-rows_out // LANES) * LANES
    own_basis = pad_to(out_basis, deep, wide)
    sib_basis = take(own_basis, "core", 1)
    grad_rows = jnp.concatenate(
        [own_rows_first(train_grads, x_lo, z), both_cores(query_grads)[0]], axis=0
    )
    g = gather_chips(pad_to(grad_rows, grad_rows.shape[0], deep))
    groups = (((0, 0), (1, 0), (0, 1), (0, 3)), ((1, 1), (1, 3), (0, 2), (1, 2)))

    half = in_basis.shape[0]
    count = train_acts.shape[0]
    def own_half(x, flip):
        low = (core == 0) != flip
        return jnp.where(low, x[:, :half], x[:, half:])

    sib_acts = take(own_half(train_acts, True), "core", 1)
    chip_acts = jnp.concatenate(
        [
            own_half(train_acts, False),
            own_half(both_cores(query_acts)[0], False),
            sib_acts,
            own_half(both_cores(query_acts)[1], False),
        ],
        axis=0,
    )
    acts = lax.all_gather(chip_acts, TENSOR)
    chips = [(h, d) for h in range(2) for d in range(4)]

    query_parts = {}
    partial = []
    for group in groups:
        *pieces, query = rotate([g[c] for c in group], own_basis, sib_basis)
        query_parts.update((c, query[s]) for s, c in enumerate(group))
        partial.append(pieces)
    bases = gather_chips(after(in_basis, partial[0][0]), partial[1][0])
    sums = []
    rotated = []
    for near, up, down, far_own, far_sib in partial:
        up = up.at[0].add(take(far_own, "z", -1))
        down = down.at[1].add(take(far_sib, "z", 1))
        kept, other = sum_z(near, take(up, "z", -1), take(down, "z", 1))
        sums.append(kept)
        mean = (kept + take(other, "x_lo", 1)).astype(jnp.bfloat16)
        near = [mean] + [take(mean, "z", d) for d in (1, 2, 3)]
        rotated.append(near + [take(jnp.stack(near), "x_lo", 1)])

    order = jnp.stack([(x_hi ^ h) * 4 + (y + d) % 4 for h, d in chips]).astype(jnp.int32)
    kept, other = rotate_acts(order, after(acts, sums[0]), [bases[c] for c in chips])
    rot_acts = (kept + take(other, "core", 1)).astype(jnp.bfloat16)
    rot_acts = jnp.concatenate(
        [own_rows_first(rot_acts[:count], x_lo, z), rot_acts[count:]], axis=0
    )
    shards = gather_chips(rot_acts)

    query_partial = jnp.concatenate([query_parts[c] for c in chips], axis=0)
    pieces = own_rows_first(after(query_partial, sums[0]), x_lo, z).reshape(4, 2, ROWS, -1)
    pieces = pieces[0] + sum(take(pieces[d], "z", -d) for d in (1, 2, 3))
    query_own = (pieces[0] + take(pieces[1], "x_lo", 1)).astype(jnp.bfloat16)
    query_near = jnp.stack([query_own] + [take(query_own, "z", d) for d in (1, 2, 3)])
    query_far = take(query_near, "x_lo", 1)
    query_acts_all = jnp.concatenate([shards[c][count:] for c in chips], axis=0)
    query_acts_all = own_rows_first(after(query_acts_all, sums[1]), x_lo, z).reshape(4, 2, ROWS, -1)
    query_len = 4 * ROWS
    divisor = query_len * (pad_to(eigvals, wide, eigvals.shape[1], value=1.0) + damping)
    precond = []
    for dx, part in enumerate((query_near, query_far)):
        numerator = jnp.dot(
            part.reshape(query_len, -1).T,
            query_acts_all[:, dx].reshape(query_len, -1),
            preferred_element_type=jnp.float32,
        )
        precond.append((numerator / divisor).astype(jnp.bfloat16))
    own_precond = jnp.stack(precond)
    sib_precond = take(own_precond, "core", 1)

    scores = {}
    for group, blocks in zip(groups, rotated):
        result = score(blocks, [shards[c] for c in group], own_precond, sib_precond)
        scores.update((c, result[:, :, s]) for s, c in enumerate(group))
    stacked = jnp.stack([scores[c] for c in chips]).reshape(2, 4, 2, 4, ROWS, QUERIES)
    stacked = stacked.transpose(5, 0, 1, 2, 3, 4)
    stacked = jnp.where(x_lo != x_hi, stacked[::-1], stacked)
    stacked = jnp.where(x_hi == 1, stacked[:, ::-1], stacked)
    stacked = jnp.where(x_lo == 1, stacked[:, :, :, ::-1], stacked)
    stacked = turn(turn(stacked, 2, (-y) % 4), 4, (-z) % 4)
    by_sequence = stacked.reshape(QUERIES, 8, SEQLEN).transpose(1, 0, 2)
    by_core = jnp.stack([jnp.where(core == c, by_sequence, 0.0) for c in range(2)], axis=1)
    spread = jnp.broadcast_to(by_core[:, :, None], (8, 2, 8, QUERIES, SEQLEN))
    received = lax.all_to_all(spread.reshape(128, QUERIES, SEQLEN), AXES, 0, 0, tiled=True)
    raw = jnp.sum(received, axis=0)
    valid = (jnp.arange(SEQLEN, dtype=jnp.int32) < lengths[0]).astype(jnp.float32)
    masked = raw * valid[None, :]
    seq_scores = jnp.sum(masked, axis=1, keepdims=True)
    token_scores = lax.dynamic_slice_in_dim(masked, (x_lo * 4 + z) * ROWS, ROWS, axis=1)
    return (token_scores, seq_scores)


def solution(mesh):
    grid = jax.sharding.Mesh(mesh.devices.reshape(SIZES), AXES)
    dp = AXES[:3]
    return jax.shard_map(
        per_device,
        mesh=grid,
        in_specs=(
            P(dp, TENSOR),
            P(dp, TENSOR),
            P(dp, TENSOR),
            P(dp, TENSOR),
            P(dp, TENSOR),
            P(TENSOR, dp),
            P(dp, TENSOR),
            P(dp),
        ),
        out_specs=(P(None, dp + TENSOR), P(None, dp)),
        check_vma=False,
    )
```

```python
import jax
import jax.numpy as jnp
from jax import lax
from jax.experimental import pallas as pl
from jax.experimental.pallas import tpu as pltpu
from jax.sharding import PartitionSpec as P

SEQLEN = 128
QUERIES = 2
AXES = ("x_hi", "y", "core", "x_lo", "z")
CHIPS = ("x_hi", "y")
TENSOR = ("x_lo", "z")
SIZES = (2, 4, 2, 2, 4)
ROWS = 16
LANES = 128
GROUP = 4
VMEM = pl.BlockSpec(memory_space=pltpu.VMEM)
SMEM = pl.BlockSpec(memory_space=pltpu.SMEM)


def params(mib):
    return pltpu.CompilerParams(vmem_limit_bytes=mib * 1024 * 1024)


damping = 0.1


def take(x, axis, step):
    count = lax.axis_size(axis)
    return lax.ppermute(x, axis, [(i, (i - step) % count) for i in range(count)])


def after(x, *earlier):
    return lax.optimization_barrier((x,) + earlier)[0]


def turn(blocks, axis, shift):
    count = blocks.shape[axis]
    return lax.dynamic_slice_in_dim(
        jnp.concatenate([blocks, blocks], axis=axis), shift, count, axis=axis
    )


def pick_kernel(order, blocks, out):
    for i in range(out.shape[0]):
        out[i] = blocks[order[i]]


def pick(order, blocks):
    return pl.pallas_call(
        pick_kernel,
        out_shape=jax.ShapeDtypeStruct(blocks.shape, blocks.dtype),
        in_specs=[SMEM, VMEM],
        out_specs=VMEM,
        compiler_params=params(6),
        name="pick",
    )(order, blocks)


def own_rows_first(rows, x_lo, z):
    order = jnp.stack([(x_lo ^ dx) * 4 + (z + dz) % 4 for dz in range(4) for dx in range(2)])
    return pick(order.astype(jnp.int32), rows.reshape(8, ROWS, -1)).reshape(rows.shape)


def both_cores(x):
    x = x.astype(jnp.float32)
    other = take(x, "core", 1)
    one, two = lax.optimization_barrier(
        (jnp.concatenate([x, other], axis=0), jnp.concatenate([other, x], axis=0))
    )
    return one.astype(jnp.bfloat16), two.astype(jnp.bfloat16)


def rotate_kernel(g0, g1, g2, g3, own_basis, sib_basis, near, up, down, far_own, far_sib, query):
    rows = jnp.concatenate([g0[...], g1[...], g2[...], g3[...]], axis=0)
    shard = g0.shape[0]
    for block, basis in enumerate((own_basis, sib_basis)):
        product = jnp.dot(rows, basis[...], preferred_element_type=jnp.float32)
        for dz in range(4):
            for dx in range(2):
                for s in range(GROUP):
                    start = s * shard + (dz * 2 + dx) * ROWS
                    piece = product[start : start + ROWS]
                    at = (dx * GROUP + s) * ROWS
                    if dz == 2:
                        target = (far_own, far_sib)[block]
                        target[at : at + ROWS, :] = piece
                    else:
                        target = (near, up, None, down)[dz]
                        target[block, at : at + ROWS, :] = piece
        if block == 0:
            for s in range(GROUP):
                start = s * shard + SEQLEN
                query[s] = product[start : start + ROWS]


def rotate(shards, own_basis, sib_basis):
    width = own_basis.shape[1]
    pair = jax.ShapeDtypeStruct((2, 2 * GROUP * ROWS, width), jnp.float32)
    single = jax.ShapeDtypeStruct((2 * GROUP * ROWS, width), jnp.float32)
    query = jax.ShapeDtypeStruct((GROUP, ROWS, width), jnp.float32)
    return pl.pallas_call(
        rotate_kernel,
        out_shape=(pair, pair, pair, single, single, query),
        in_specs=[VMEM] * 6,
        out_specs=(VMEM,) * 6,
        compiler_params=params(24),
        cost_estimate=pl.CostEstimate(
            flops=2 * 576 * 1728 * 1728, bytes_accessed=12 * 1024 * 1024, transcendentals=0
        ),
        name="rotate",
    )(*shards, own_basis, sib_basis)


def sum_z_kernel(near, up, down, kept, other):
    half = GROUP * ROWS
    for block in range(2):
        total = near[block] + up[block] + down[block]
        kept[block] = total[:half]
        other[block] = total[half:]


def sum_z(*arrays):
    width = arrays[0].shape[2]
    part = jax.ShapeDtypeStruct((2, GROUP * ROWS, width), jnp.float32)
    return pl.pallas_call(
        sum_z_kernel,
        out_shape=(part, part),
        in_specs=[VMEM] * 3,
        out_specs=(VMEM, VMEM),
        compiler_params=params(10),
        cost_estimate=pl.CostEstimate(
            flops=4 * 64 * 864, bytes_accessed=2 * 1024 * 1024, transcendentals=0
        ),
        name="sum_z",
    )(*arrays)


def score_kernel(*refs):
    blocks, acts, (own_precond, sib_precond, out) = refs[:-7], refs[-7:-3], refs[-3:]
    if len(blocks) == 5:
        place = [b for b in blocks[:4]] + [blocks[4].at[i] for i in range(4)]
    else:
        place = [b.at[dx] for dx in range(2) for b in blocks]
    own = jnp.concatenate([b[0] for b in place], axis=0)
    sib = jnp.concatenate([b[1] for b in place], axis=0)
    acts = [x[...].astype(jnp.float32) for x in acts]
    wide = []
    for dx in range(2):
        for dz in range(4):
            start = (dz * 2 + dx) * ROWS
            wide += [x[start : start + ROWS] for x in acts]
    wide = jnp.concatenate(wide, axis=0)
    for k in range(QUERIES):
        projected = jnp.dot(own, own_precond[k], preferred_element_type=jnp.float32)
        projected += jnp.dot(sib, sib_precond[k], preferred_element_type=jnp.float32)
        out[:, k : k + 1] = jnp.sum(projected * wide, axis=1, keepdims=True)


def score(blocks, acts, own_precond, sib_precond):
    out = pl.pallas_call(
        score_kernel,
        out_shape=jax.ShapeDtypeStruct((GROUP * SEQLEN, QUERIES), jnp.float32),
        in_specs=[VMEM] * (len(blocks) + 6),
        out_specs=VMEM,
        compiler_params=params(20),
        cost_estimate=pl.CostEstimate(
            flops=2 * 512 * 1728 * 1280, bytes_accessed=8 * 1024 * 1024, transcendentals=0
        ),
        name="score",
    )(*blocks, *acts, own_precond, sib_precond)
    return out.reshape(2, 4, GROUP, ROWS, QUERIES)


def act_kernel(order, acts, *refs):
    bases, (kept, other) = refs[:8], refs[8:]
    total = jnp.zeros((acts.shape[1], kept.shape[1]), jnp.float32)
    for m in range(8):
        total += jnp.dot(acts[order[m]], bases[m][...], preferred_element_type=jnp.float32)
    half = acts.shape[1] // 2
    kept[...] = total[:half]
    other[...] = total[half:]


def rotate_acts(order, acts, bases):
    part = jax.ShapeDtypeStruct((acts.shape[1] // 2, bases[0].shape[1]), jnp.float32)
    return pl.pallas_call(
        act_kernel,
        out_shape=(part, part),
        in_specs=[SMEM] + [VMEM] * 9,
        out_specs=(VMEM, VMEM),
        compiler_params=params(12),
        cost_estimate=pl.CostEstimate(
            flops=2 * 288 * 2560 * 640, bytes_accessed=6 * 1024 * 1024, transcendentals=0
        ),
        name="rotate_acts",
    )(order, acts, *bases)


def pad_to(x, *shape, value=0):
    return jnp.pad(x, [(0, n - m) for m, n in zip(x.shape, shape)], constant_values=value)


def per_device(
    train_acts, train_grads, query_acts, query_grads, in_basis, out_basis, eigvals, lengths
):
    x_hi = lax.axis_index("x_hi")
    y = lax.axis_index("y")
    core = lax.axis_index("core")
    x_lo = lax.axis_index("x_lo")
    z = lax.axis_index("z")

    half = in_basis.shape[0]
    count = train_acts.shape[0]
    def own_half(x, flip):
        low = (core == 0) != flip
        return jnp.where(low, x[:, :half], x[:, half:])

    sib_acts = take(own_half(train_acts, True), "core", 1)
    chip_acts = jnp.concatenate(
        [
            own_half(train_acts, False),
            own_half(both_cores(query_acts)[0], False),
            sib_acts,
            own_half(both_cores(query_acts)[1], False),
        ],
        axis=0,
    )
    sync = lax.optimization_barrier
    rows_in, rows_out = out_basis.shape
    deep = -(-rows_in // LANES) * LANES
    wide = -(-rows_out // LANES) * LANES
    own_basis = pad_to(out_basis, deep, wide)
    grad_rows = jnp.concatenate(
        [own_rows_first(train_grads, x_lo, z), both_cores(query_grads)[0]], axis=0
    )
    g = {(0, 0): pad_to(grad_rows, grad_rows.shape[0], deep)}
    g[1, 0] = take(g[0, 0], "x_hi", 1)
    g[0, 1] = take(g[0, 0], "y", 1)
    g[0, 3] = take(g[0, 0], "y", -1)
    sib_basis = take(own_basis, "core", 1)
    acts_z = [take(chip_acts, "z", d) for d in (1, 2, 3)]
    g[1, 0], g[0, 1], g[0, 3], sib_basis, acts_z = sync(
        (g[1, 0], g[0, 1], g[0, 3], sib_basis, acts_z)
    )
    chips = [(h, d) for h in range(2) for d in range(4)]
    groups = (((0, 0), (1, 0), (0, 1), (0, 3)), ((1, 1), (1, 3), (0, 2), (1, 2)))

    g[1, 1] = take(g[1, 0], "y", 1)
    g[1, 3] = take(g[1, 0], "y", -1)
    near_1, up_1, down_1, far_own, far_sib, query_1 = rotate(
        [g[c] for c in groups[0]], own_basis, sib_basis
    )
    g[1, 1], g[1, 3], near_1, up_1, down_1, far_own, far_sib, query_1 = sync(
        (g[1, 1], g[1, 3], near_1, up_1, down_1, far_own, far_sib, query_1)
    )

    far_own, far_sib = take(far_own, "z", -1), take(far_sib, "z", 1)
    g[0, 2] = take(g[0, 1], "y", 1)
    g[1, 2] = take(g[1, 3], "y", -1)
    acts_near = jnp.stack([chip_acts] + acts_z)
    acts_far = take(acts_near, "x_lo", 1)
    far_own, far_sib, g[0, 2], g[1, 2] = sync((far_own, far_sib, g[0, 2], g[1, 2]))

    up_1 = take(up_1.at[0].add(far_own), "z", -1)
    down_1 = take(down_1.at[1].add(far_sib), "z", 1)
    v = {(0, 0): sync((in_basis, g[1, 2]))[0]}
    v[1, 0] = take(v[0, 0], "x_hi", 1)
    v[0, 1] = take(v[0, 0], "y", 1)
    v[0, 3] = take(v[0, 0], "y", -1)
    near_2, up_2, down_2, far_own, far_sib, query_2 = rotate(
        [g[c] for c in groups[1]], own_basis, sib_basis
    )
    far_own, far_sib = take(far_own, "z", -1), take(far_sib, "z", 1)
    query_parts = {c: query_1[s] for s, c in enumerate(groups[0])}
    query_parts.update((c, query_2[s]) for s, c in enumerate(groups[1]))
    query_partial = jnp.concatenate([query_parts[c] for c in chips], axis=0)
    pieces = own_rows_first(query_partial, x_lo, z).reshape(4, 2, ROWS, -1)
    query_z = [take(pieces[d], "z", -d) for d in (1, 2, 3)]
    (up_1, down_1, v[1, 0], v[0, 1], v[0, 3], near_2, up_2, down_2, far_own, far_sib, query_z, acts_far) = sync(
        (up_1, down_1, v[1, 0], v[0, 1], v[0, 3], near_2, up_2, down_2, far_own, far_sib, query_z, acts_far)
    )

    up_2 = take(up_2.at[0].add(far_own), "z", -1)
    down_2 = take(down_2.at[1].add(far_sib), "z", 1)
    kept_1, other_1 = sum_z(near_1, up_1, down_1)
    other_1 = take(other_1, "x_lo", 1)
    v[1, 1] = take(v[1, 0], "y", 1)
    v[1, 3] = take(v[1, 0], "y", -1)
    v[0, 2] = take(v[0, 1], "y", 1)
    v[1, 2] = take(v[1, 3], "y", -1)
    pieces = pieces[0] + query_z[0] + query_z[1] + query_z[2]
    query_x = take(pieces[1], "x_lo", 1)
    acts = jnp.concatenate([acts_near, acts_far], axis=0)
    (up_2, down_2, kept_1, other_1, v[1, 1], v[1, 3], v[0, 2], v[1, 2], query_x, acts) = sync(
        (up_2, down_2, kept_1, other_1, v[1, 1], v[1, 3], v[0, 2], v[1, 2], query_x, acts)
    )

    mean_1 = (kept_1 + other_1).astype(jnp.bfloat16)
    kept_2, other_2 = sum_z(near_2, up_2, down_2)
    other_2 = take(other_2, "x_lo", 1)
    near_1 = [take(mean_1, "z", d) for d in (1, 2, 3)]
    order = jnp.stack([(x_lo ^ x_hi ^ h) * 4 + (y - z + d) % 4 for h, d in chips])
    kept, other = rotate_acts(order.astype(jnp.int32), acts, [v[c] for c in chips])
    rot_acts = (kept + take(other, "core", 1)).astype(jnp.bfloat16)
    rot_acts = jnp.concatenate(
        [own_rows_first(rot_acts[:count], x_lo, z), rot_acts[count:]], axis=0
    )
    r = {(0, 0): rot_acts}
    r[1, 0] = take(r[0, 0], "x_hi", 1)
    r[0, 1] = take(r[0, 0], "y", 1)
    r[0, 3] = take(r[0, 0], "y", -1)
    query_own = (pieces[0] + query_x).astype(jnp.bfloat16)
    query_near = [take(query_own, "z", d) for d in (1, 2, 3)]
    kept_2, other_2, near_1, r[1, 0], r[0, 1], r[0, 3], query_near = sync(
        (kept_2, other_2, near_1, r[1, 0], r[0, 1], r[0, 3], query_near)
    )

    mean_2 = (kept_2 + other_2).astype(jnp.bfloat16)
    pair_2 = take(mean_2, "x_lo", 1)
    query_near = jnp.stack([query_own] + query_near)
    query_far = take(query_near, "x_lo", 1)
    r[1, 1] = take(r[1, 0], "y", 1)
    r[1, 3] = take(r[1, 0], "y", -1)
    r[0, 2] = take(r[0, 1], "y", 1)
    r[1, 2] = take(r[1, 3], "y", -1)
    near_1 = [mean_1] + near_1
    near_1_all = jnp.stack(near_1)
    pair_2, query_far, r[1, 1], r[1, 3], r[0, 2], r[1, 2], near_1_all = sync(
        (pair_2, query_far, r[1, 1], r[1, 3], r[0, 2], r[1, 2], near_1_all)
    )

    far_1 = take(near_1_all, "x_lo", 1)
    pair_2 = jnp.stack([mean_2, pair_2])
    pairs_2 = [pair_2] + [take(pair_2, "z", d) for d in (1, 2, 3)]
    query_acts_all = jnp.concatenate([r[c][count:] for c in chips], axis=0)
    query_acts_all = own_rows_first(query_acts_all, x_lo, z).reshape(4, 2, ROWS, -1)
    query_len = 4 * ROWS
    divisor = query_len * (pad_to(eigvals, wide, eigvals.shape[1], value=1.0) + damping)
    precond = []
    for dx, part in enumerate((query_near, query_far)):
        numerator = jnp.dot(
            part.reshape(query_len, -1).T,
            query_acts_all[:, dx].reshape(query_len, -1),
            preferred_element_type=jnp.float32,
        )
        precond.append((numerator / divisor).astype(jnp.bfloat16))
    own_precond = jnp.stack(precond)
    sib_precond = take(own_precond, "core", 1)
    far_1, pairs_2, sib_precond = sync((far_1, pairs_2, sib_precond))
    shards = r
    rotated = (near_1 + [far_1], pairs_2)

    scores = {}
    for group, blocks in zip(groups, rotated):
        result = score(blocks, [shards[c] for c in group], own_precond, sib_precond)
        scores.update((c, result[:, :, s]) for s, c in enumerate(group))
    stacked = jnp.stack([scores[c] for c in chips]).reshape(2, 4, 2, 4, ROWS, QUERIES)
    stacked = stacked.transpose(5, 0, 1, 2, 3, 4)
    stacked = jnp.where(x_lo != x_hi, stacked[::-1], stacked)
    stacked = jnp.where(x_hi == 1, stacked[:, ::-1], stacked)
    stacked = jnp.where(x_lo == 1, stacked[:, :, :, ::-1], stacked)
    stacked = turn(turn(stacked, 2, (-y) % 4), 4, (-z) % 4)
    by_sequence = stacked.reshape(QUERIES, 8, SEQLEN).transpose(1, 0, 2)
    by_core = jnp.stack([jnp.where(core == c, by_sequence, 0.0) for c in range(2)], axis=1)
    spread = jnp.broadcast_to(by_core[:, :, None], (8, 2, 8, QUERIES, SEQLEN))
    received = lax.all_to_all(spread.reshape(128, QUERIES, SEQLEN), AXES, 0, 0, tiled=True)
    raw = jnp.sum(received, axis=0)
    valid = (jnp.arange(SEQLEN, dtype=jnp.int32) < lengths[0]).astype(jnp.float32)
    masked = raw * valid[None, :]
    seq_scores = jnp.sum(masked, axis=1, keepdims=True)
    token_scores = lax.dynamic_slice_in_dim(masked, (x_lo * 4 + z) * ROWS, ROWS, axis=1)
    return (token_scores, seq_scores)


def solution(mesh):
    grid = jax.sharding.Mesh(mesh.devices.reshape(SIZES), AXES)
    dp = AXES[:3]
    return jax.shard_map(
        per_device,
        mesh=grid,
        in_specs=(
            P(dp, TENSOR),
            P(dp, TENSOR),
            P(dp, TENSOR),
            P(dp, TENSOR),
            P(dp, TENSOR),
            P(TENSOR, dp),
            P(dp, TENSOR),
            P(dp),
        ),
        out_specs=(P(None, dp + TENSOR), P(None, dp)),
        check_vma=False,
    )
```

```python
import jax
import jax.numpy as jnp
from jax import lax
from jax.experimental import pallas as pl
from jax.experimental.pallas import tpu as pltpu
from jax.sharding import PartitionSpec as P

SEQLEN = 128
QUERIES = 2
AXES = ("x_hi", "y", "core", "x_lo", "z")
CHIPS = ("x_hi", "y")
TENSOR = ("x_lo", "z")
SIZES = (2, 4, 2, 2, 4)
ROWS = 16
LANES = 128
GROUP = 4
VMEM = pl.BlockSpec(memory_space=pltpu.VMEM)
SMEM = pl.BlockSpec(memory_space=pltpu.SMEM)


def params(mib):
    return pltpu.CompilerParams(vmem_limit_bytes=mib * 1024 * 1024)


damping = 0.1


def take(x, axis, step):
    count = lax.axis_size(axis)
    return lax.ppermute(x, axis, [(i, (i - step) % count) for i in range(count)])


def after(x, *earlier):
    return lax.optimization_barrier((x,) + earlier)[0]


def turn(blocks, axis, shift):
    count = blocks.shape[axis]
    return lax.dynamic_slice_in_dim(
        jnp.concatenate([blocks, blocks], axis=axis), shift, count, axis=axis
    )


def pick_kernel(order, blocks, out):
    for i in range(out.shape[0]):
        out[i] = blocks[order[i]]


def pick(order, blocks):
    return pl.pallas_call(
        pick_kernel,
        out_shape=jax.ShapeDtypeStruct(blocks.shape, blocks.dtype),
        in_specs=[SMEM, VMEM],
        out_specs=VMEM,
        compiler_params=params(6),
        name="pick",
    )(order, blocks)


def own_rows_first(rows, x_lo, z):
    order = jnp.stack([(x_lo ^ dx) * 4 + (z + dz) % 4 for dz in range(4) for dx in range(2)])
    return pick(order.astype(jnp.int32), rows.reshape(8, ROWS, -1)).reshape(rows.shape)


def both_cores(x):
    x = x.astype(jnp.float32)
    other = take(x, "core", 1)
    one, two = lax.optimization_barrier(
        (jnp.concatenate([x, other], axis=0), jnp.concatenate([other, x], axis=0))
    )
    return one.astype(jnp.bfloat16), two.astype(jnp.bfloat16)


def rotate_kernel(g0, g1, g2, g3, own_basis, sib_basis, near, up, down, far_own, far_sib, query):
    rows = jnp.concatenate([g0[...], g1[...], g2[...], g3[...]], axis=0)
    shard = g0.shape[0]
    for block, basis in enumerate((own_basis, sib_basis)):
        product = jnp.dot(rows, basis[...], preferred_element_type=jnp.float32)
        for dz in range(4):
            for dx in range(2):
                for s in range(GROUP):
                    start = s * shard + (dz * 2 + dx) * ROWS
                    piece = product[start : start + ROWS]
                    at = (dx * GROUP + s) * ROWS
                    if dz == 2:
                        target = (far_own, far_sib)[block]
                        target[at : at + ROWS, :] = piece
                    else:
                        target = (near, up, None, down)[dz]
                        target[block, at : at + ROWS, :] = piece
        if block == 0:
            for s in range(GROUP):
                start = s * shard + SEQLEN
                query[s] = product[start : start + ROWS]


def rotate(shards, own_basis, sib_basis):
    width = own_basis.shape[1]
    pair = jax.ShapeDtypeStruct((2, 2 * GROUP * ROWS, width), jnp.float32)
    single = jax.ShapeDtypeStruct((2 * GROUP * ROWS, width), jnp.float32)
    query = jax.ShapeDtypeStruct((GROUP, ROWS, width), jnp.float32)
    return pl.pallas_call(
        rotate_kernel,
        out_shape=(pair, pair, pair, single, single, query),
        in_specs=[VMEM] * 6,
        out_specs=(VMEM,) * 6,
        compiler_params=params(24),
        cost_estimate=pl.CostEstimate(
            flops=2 * 576 * 1728 * 1728, bytes_accessed=12 * 1024 * 1024, transcendentals=0
        ),
        name="rotate",
    )(*shards, own_basis, sib_basis)


def sum_z_kernel(near, up, down, kept, other):
    half = GROUP * ROWS
    for block in range(2):
        total = near[block] + up[block] + down[block]
        kept[block] = total[:half]
        other[block] = total[half:]


def sum_z(*arrays):
    width = arrays[0].shape[2]
    part = jax.ShapeDtypeStruct((2, GROUP * ROWS, width), jnp.float32)
    return pl.pallas_call(
        sum_z_kernel,
        out_shape=(part, part),
        in_specs=[VMEM] * 3,
        out_specs=(VMEM, VMEM),
        compiler_params=params(10),
        cost_estimate=pl.CostEstimate(
            flops=4 * 64 * 864, bytes_accessed=2 * 1024 * 1024, transcendentals=0
        ),
        name="sum_z",
    )(*arrays)


def score_kernel(*refs):
    blocks, acts, (own_precond, sib_precond, out) = refs[:-7], refs[-7:-3], refs[-3:]
    if len(blocks) == 2:
        place = [b.at[i] for b in blocks for i in range(4)]
    else:
        place = [b.at[dx] for dx in range(2) for b in blocks]
    own = jnp.concatenate([b[0] for b in place], axis=0)
    sib = jnp.concatenate([b[1] for b in place], axis=0)
    if len(blocks) == 2:
        acts = (acts[0][0], acts[0][1], acts[1][0], acts[3][0])
    else:
        acts = (acts[1][1], acts[3][1], acts[2][0], acts[2][1])
    acts = [x.astype(jnp.float32) for x in acts]
    wide = []
    for dx in range(2):
        for dz in range(4):
            start = (dz * 2 + dx) * ROWS
            wide += [x[start : start + ROWS] for x in acts]
    wide = jnp.concatenate(wide, axis=0)
    for k in range(QUERIES):
        projected = jnp.dot(own, own_precond[k], preferred_element_type=jnp.float32)
        projected += jnp.dot(sib, sib_precond[k], preferred_element_type=jnp.float32)
        out[:, k : k + 1] = jnp.sum(projected * wide, axis=1, keepdims=True)


def score(blocks, acts, own_precond, sib_precond):
    out = pl.pallas_call(
        score_kernel,
        out_shape=jax.ShapeDtypeStruct((GROUP * SEQLEN, QUERIES), jnp.float32),
        in_specs=[VMEM] * (len(blocks) + 6),
        out_specs=VMEM,
        compiler_params=params(20),
        cost_estimate=pl.CostEstimate(
            flops=2 * 512 * 1728 * 1280, bytes_accessed=8 * 1024 * 1024, transcendentals=0
        ),
        name="score",
    )(*blocks, *acts, own_precond, sib_precond)
    return out.reshape(2, 4, GROUP, ROWS, QUERIES)


def act_kernel(order, acts, *refs):
    bases, (kept, other) = refs[:8], refs[8:]
    total = jnp.zeros((acts.shape[1], kept.shape[1]), jnp.float32)
    for m in range(8):
        total += jnp.dot(acts[order[m]], bases[m][...], preferred_element_type=jnp.float32)
    half = acts.shape[1] // 2
    kept[...] = total[:half]
    other[...] = total[half:]


def rotate_acts(order, acts, bases):
    part = jax.ShapeDtypeStruct((acts.shape[1] // 2, bases[0].shape[1]), jnp.float32)
    return pl.pallas_call(
        act_kernel,
        out_shape=(part, part),
        in_specs=[SMEM] + [VMEM] * 9,
        out_specs=(VMEM, VMEM),
        compiler_params=params(12),
        cost_estimate=pl.CostEstimate(
            flops=2 * 288 * 2560 * 640, bytes_accessed=6 * 1024 * 1024, transcendentals=0
        ),
        name="rotate_acts",
    )(order, acts, *bases)


def pad_to(x, *shape, value=0):
    return jnp.pad(x, [(0, n - m) for m, n in zip(x.shape, shape)], constant_values=value)


def per_device(
    train_acts, train_grads, query_acts, query_grads, in_basis, out_basis, eigvals, lengths
):
    x_hi = lax.axis_index("x_hi")
    y = lax.axis_index("y")
    core = lax.axis_index("core")
    x_lo = lax.axis_index("x_lo")
    z = lax.axis_index("z")

    half = in_basis.shape[0]
    count = train_acts.shape[0]
    def own_half(x, flip):
        low = (core == 0) != flip
        return jnp.where(low, x[:, :half], x[:, half:])

    sib_acts = take(own_half(train_acts, True), "core", 1)
    chip_acts = jnp.concatenate(
        [
            own_half(train_acts, False),
            own_half(both_cores(query_acts)[0], False),
            sib_acts,
            own_half(both_cores(query_acts)[1], False),
        ],
        axis=0,
    )
    sync = lax.optimization_barrier
    rows_in, rows_out = out_basis.shape
    deep = -(-rows_in // LANES) * LANES
    wide = -(-rows_out // LANES) * LANES
    own_basis = pad_to(out_basis, deep, wide)
    grad_rows = jnp.concatenate(
        [own_rows_first(train_grads, x_lo, z), both_cores(query_grads)[0]], axis=0
    )
    g = {(0, 0): pad_to(grad_rows, grad_rows.shape[0], deep)}
    g[1, 0] = take(g[0, 0], "x_hi", 1)
    g[0, 1] = take(g[0, 0], "y", 1)
    g[0, 3] = take(g[0, 0], "y", -1)
    sib_basis = take(own_basis, "core", 1)
    acts_z = [take(chip_acts, "z", d) for d in (1, 2, 3)]
    g[1, 0], g[0, 1], g[0, 3], sib_basis, acts_z = sync(
        (g[1, 0], g[0, 1], g[0, 3], sib_basis, acts_z)
    )
    chips = [(h, d) for h in range(2) for d in range(4)]
    groups = (((0, 0), (1, 0), (0, 1), (0, 3)), ((1, 1), (1, 3), (0, 2), (1, 2)))

    g[1, 1] = take(g[1, 0], "y", 1)
    g[1, 3] = take(g[1, 0], "y", -1)
    near_1, up_1, down_1, far_own, far_sib, query_1 = rotate(
        [g[c] for c in groups[0]], own_basis, sib_basis
    )

    far_own, far_sib = take(far_own, "z", -1), take(far_sib, "z", 1)
    g[0, 2] = take(g[0, 1], "y", 1)
    g[1, 2] = take(g[1, 3], "y", -1)
    acts_near = jnp.stack([chip_acts] + acts_z)
    acts_far = take(acts_near, "x_lo", 1)
    far_own, far_sib, g[0, 2], g[1, 2] = sync((far_own, far_sib, g[0, 2], g[1, 2]))

    up_1 = take(up_1.at[0].add(far_own), "z", -1)
    down_1 = take(down_1.at[1].add(far_sib), "z", 1)
    v = {(0, 0): sync((in_basis, g[1, 2]))[0]}
    v[1, 0] = take(v[0, 0], "x_hi", 1)
    v[0, 1] = take(v[0, 0], "y", 1)
    v[0, 3] = take(v[0, 0], "y", -1)
    near_2, up_2, down_2, far_own, far_sib, query_2 = rotate(
        [g[c] for c in groups[1]], own_basis, sib_basis
    )
    far_own, far_sib = take(far_own, "z", -1), take(far_sib, "z", 1)
    query_parts = {c: query_1[s] for s, c in enumerate(groups[0])}
    query_parts.update((c, query_2[s]) for s, c in enumerate(groups[1]))
    query_partial = jnp.concatenate([query_parts[c] for c in chips], axis=0)
    pieces = own_rows_first(query_partial, x_lo, z).reshape(4, 2, ROWS, -1)
    query_z = [take(pieces[d], "z", -d) for d in (1, 2, 3)]
    (up_1, down_1, v[1, 0], v[0, 1], v[0, 3], near_2, up_2, down_2, far_own, far_sib, query_z, acts_far) = sync(
        (up_1, down_1, v[1, 0], v[0, 1], v[0, 3], near_2, up_2, down_2, far_own, far_sib, query_z, acts_far)
    )

    up_2 = take(up_2.at[0].add(far_own), "z", -1)
    down_2 = take(down_2.at[1].add(far_sib), "z", 1)
    kept_1, other_1 = sum_z(near_1, up_1, down_1)
    other_1 = take(other_1, "x_lo", 1)
    v[1, 1] = take(v[1, 0], "y", 1)
    v[1, 3] = take(v[1, 0], "y", -1)
    v[0, 2] = take(v[0, 1], "y", 1)
    v[1, 2] = take(v[1, 3], "y", -1)
    pieces = pieces[0] + query_z[0] + query_z[1] + query_z[2]
    query_x = take(pieces[1], "x_lo", 1)
    acts = jnp.concatenate([acts_near, acts_far], axis=0)
    (up_2, down_2, kept_1, other_1, v[1, 1], v[1, 3], v[0, 2], v[1, 2], query_x, acts) = sync(
        (up_2, down_2, kept_1, other_1, v[1, 1], v[1, 3], v[0, 2], v[1, 2], query_x, acts)
    )

    mean_1 = (kept_1 + other_1).astype(jnp.bfloat16)
    kept_2, other_2 = sum_z(near_2, up_2, down_2)
    other_2 = take(other_2, "x_lo", 1)
    near_1 = [take(mean_1, "z", d) for d in (1, 2, 3)]
    order = jnp.stack([(x_lo ^ x_hi ^ h) * 4 + (y - z + d) % 4 for h, d in chips])
    kept, other = rotate_acts(order.astype(jnp.int32), acts, [v[c] for c in chips])
    rot_acts = (kept + take(other, "core", 1)).astype(jnp.bfloat16)
    rot_acts = jnp.concatenate(
        [own_rows_first(rot_acts[:count], x_lo, z), rot_acts[count:]], axis=0
    )
    pair = jnp.stack([rot_acts, take(rot_acts, "x_hi", 1)])
    query_own = (pieces[0] + query_x).astype(jnp.bfloat16)
    query_near = [take(query_own, "z", d) for d in (1, 2, 3)]

    mean_2 = (kept_2 + other_2).astype(jnp.bfloat16)
    pair_2 = take(mean_2, "x_lo", 1)
    query_near = jnp.stack([query_own] + query_near)
    query_far = take(query_near, "x_lo", 1)
    pairs = [pair, take(pair, "y", 1), take(pair, "y", 2), take(pair, "y", -1)]
    near_1 = [mean_1] + near_1
    near_1_all = jnp.stack(near_1)
    pair_2, query_far, pairs, near_1_all = sync(
        (pair_2, query_far, pairs, near_1_all)
    )

    far_1 = take(near_1_all, "x_lo", 1)
    pair_2 = jnp.stack([mean_2, pair_2])
    pairs_2 = [pair_2] + [take(pair_2, "z", d) for d in (1, 2, 3)]
    query_acts_all = jnp.concatenate([pairs[d][h, count:] for h, d in chips], axis=0)
    query_acts_all = own_rows_first(query_acts_all, x_lo, z).reshape(4, 2, ROWS, -1)
    query_len = 4 * ROWS
    divisor = query_len * (pad_to(eigvals, wide, eigvals.shape[1], value=1.0) + damping)
    precond = []
    for dx, part in enumerate((query_near, query_far)):
        numerator = jnp.dot(
            part.reshape(query_len, -1).T,
            query_acts_all[:, dx].reshape(query_len, -1),
            preferred_element_type=jnp.float32,
        )
        precond.append((numerator / divisor).astype(jnp.bfloat16))
    own_precond = jnp.stack(precond)
    sib_precond = take(own_precond, "core", 1)

    scores = {}
    result = score([near_1_all, far_1], pairs, own_precond, sib_precond)
    pairs_2, result = sync((pairs_2, result))
    for group, part in zip(groups, (result, score(pairs_2, pairs, own_precond, sib_precond))):
        scores.update((c, part[:, :, s]) for s, c in enumerate(group))
    stacked = jnp.stack([scores[c] for c in chips]).reshape(2, 4, 2, 4, ROWS, QUERIES)
    stacked = stacked.transpose(5, 0, 1, 2, 3, 4)
    stacked = jnp.where(x_lo != x_hi, stacked[::-1], stacked)
    stacked = jnp.where(x_hi == 1, stacked[:, ::-1], stacked)
    stacked = jnp.where(x_lo == 1, stacked[:, :, :, ::-1], stacked)
    stacked = turn(turn(stacked, 2, (-y) % 4), 4, (-z) % 4)
    by_sequence = stacked.reshape(QUERIES, 8, SEQLEN).transpose(1, 0, 2)
    by_core = jnp.stack([jnp.where(core == c, by_sequence, 0.0) for c in range(2)], axis=1)
    spread = jnp.broadcast_to(by_core[:, :, None], (8, 2, 8, QUERIES, SEQLEN))
    received = lax.all_to_all(spread.reshape(128, QUERIES, SEQLEN), AXES, 0, 0, tiled=True)
    raw = jnp.sum(received, axis=0)
    valid = (jnp.arange(SEQLEN, dtype=jnp.int32) < lengths[0]).astype(jnp.float32)
    masked = raw * valid[None, :]
    seq_scores = jnp.sum(masked, axis=1, keepdims=True)
    token_scores = lax.dynamic_slice_in_dim(masked, (x_lo * 4 + z) * ROWS, ROWS, axis=1)
    return (token_scores, seq_scores)


def solution(mesh):
    grid = jax.sharding.Mesh(mesh.devices.reshape(SIZES), AXES)
    dp = AXES[:3]
    return jax.shard_map(
        per_device,
        mesh=grid,
        in_specs=(
            P(dp, TENSOR),
            P(dp, TENSOR),
            P(dp, TENSOR),
            P(dp, TENSOR),
            P(dp, TENSOR),
            P(TENSOR, dp),
            P(dp, TENSOR),
            P(dp),
        ),
        out_specs=(P(None, dp + TENSOR), P(None, dp)),
        check_vma=False,
    )
```

```python
import jax
import jax.numpy as jnp
from jax import lax
from jax.experimental import pallas as pl
from jax.experimental.pallas import tpu as pltpu
from jax.sharding import PartitionSpec as P

SEQLEN = 128
QUERIES = 2
AXES = ("x_hi", "y", "core", "x_lo", "z")
CHIPS = ("x_hi", "y")
TENSOR = ("x_lo", "z")
SIZES = (2, 4, 2, 2, 4)
ROWS = 16
LANES = 128
GROUP = 4
VMEM = pl.BlockSpec(memory_space=pltpu.VMEM)
SMEM = pl.BlockSpec(memory_space=pltpu.SMEM)


def params(mib):
    return pltpu.CompilerParams(vmem_limit_bytes=mib * 1024 * 1024)


damping = 0.1


def take(x, axis, step):
    count = lax.axis_size(axis)
    return lax.ppermute(x, axis, [(i, (i - step) % count) for i in range(count)])


def after(x, *earlier):
    return lax.optimization_barrier((x,) + earlier)[0]


def turn(blocks, axis, shift):
    count = blocks.shape[axis]
    return lax.dynamic_slice_in_dim(
        jnp.concatenate([blocks, blocks], axis=axis), shift, count, axis=axis
    )


def pick_kernel(order, blocks, out):
    for i in range(out.shape[0]):
        out[i] = blocks[order[i]]


def pick(order, blocks):
    return pl.pallas_call(
        pick_kernel,
        out_shape=jax.ShapeDtypeStruct(blocks.shape, blocks.dtype),
        in_specs=[SMEM, VMEM],
        out_specs=VMEM,
        compiler_params=params(2),
        name="pick",
    )(order, blocks)


def own_rows_first(rows, x_lo, z):
    order = jnp.stack([(x_lo ^ dx) * 4 + (z + dz) % 4 for dz in range(4) for dx in range(2)])
    return pick(order.astype(jnp.int32), rows.reshape(8, ROWS, -1)).reshape(rows.shape)


def both_cores(x):
    x = x.astype(jnp.float32)
    other = take(x, "core", 1)
    one, two = lax.optimization_barrier(
        (jnp.concatenate([x, other], axis=0), jnp.concatenate([other, x], axis=0))
    )
    return one.astype(jnp.bfloat16), two.astype(jnp.bfloat16)


def rotate_kernel(g0, g1, g2, g3, own_basis, sib_basis, near, up, down, far_own, far_sib, query):
    rows = jnp.concatenate([g0[...], g1[...], g2[...], g3[...]], axis=0)
    shard = g0.shape[0]
    for block, basis in enumerate((own_basis, sib_basis)):
        product = jnp.dot(rows, basis[...], preferred_element_type=jnp.float32)
        for dz in range(4):
            for dx in range(2):
                for s in range(GROUP):
                    start = s * shard + (dz * 2 + dx) * ROWS
                    piece = product[start : start + ROWS]
                    at = (dx * GROUP + s) * ROWS
                    if dz == 2:
                        target = (far_own, far_sib)[block]
                        target[at : at + ROWS, :] = piece
                    else:
                        target = (near, up, None, down)[dz]
                        target[block, at : at + ROWS, :] = piece
        if block == 0:
            for s in range(GROUP):
                start = s * shard + SEQLEN
                query[s] = product[start : start + ROWS]


def rotate(shards, own_basis, sib_basis):
    width = own_basis.shape[1]
    pair = jax.ShapeDtypeStruct((2, 2 * GROUP * ROWS, width), jnp.float32)
    single = jax.ShapeDtypeStruct((2 * GROUP * ROWS, width), jnp.float32)
    query = jax.ShapeDtypeStruct((GROUP, ROWS, width), jnp.float32)
    return pl.pallas_call(
        rotate_kernel,
        out_shape=(pair, pair, pair, single, single, query),
        in_specs=[VMEM] * 6,
        out_specs=(VMEM,) * 6,
        compiler_params=params(18),
        cost_estimate=pl.CostEstimate(
            flops=2 * 576 * 1728 * 1728, bytes_accessed=12 * 1024 * 1024, transcendentals=0
        ),
        name="rotate",
    )(*shards, own_basis, sib_basis)


def sum_z_kernel(near, up, down, kept, other):
    half = GROUP * ROWS
    for block in range(2):
        total = near[block] + up[block] + down[block]
        kept[block] = total[:half]
        other[block] = total[half:]


def sum_z(*arrays):
    width = arrays[0].shape[2]
    part = jax.ShapeDtypeStruct((2, GROUP * ROWS, width), jnp.float32)
    return pl.pallas_call(
        sum_z_kernel,
        out_shape=(part, part),
        in_specs=[VMEM] * 3,
        out_specs=(VMEM, VMEM),
        compiler_params=params(6),
        cost_estimate=pl.CostEstimate(
            flops=4 * 64 * 864, bytes_accessed=2 * 1024 * 1024, transcendentals=0
        ),
        name="sum_z",
    )(*arrays)


def score_kernel(*refs):
    blocks, acts, (own_precond, sib_precond, out) = refs[:-7], refs[-7:-3], refs[-3:]
    if len(blocks) == 2:
        place = [b.at[i] for b in blocks for i in range(4)]
    else:
        place = [b.at[dx] for dx in range(2) for b in blocks]
    own = jnp.concatenate([b[0] for b in place], axis=0)
    sib = jnp.concatenate([b[1] for b in place], axis=0)
    if len(blocks) == 2:
        acts = (acts[0][0], acts[0][1], acts[1][0], acts[3][0])
    else:
        acts = (acts[1][1], acts[3][1], acts[2][0], acts[2][1])
    acts = [x.astype(jnp.float32) for x in acts]
    wide = []
    for dx in range(2):
        for dz in range(4):
            start = (dz * 2 + dx) * ROWS
            wide += [x[start : start + ROWS] for x in acts]
    wide = jnp.concatenate(wide, axis=0)
    for k in range(QUERIES):
        projected = jnp.dot(own, own_precond[k], preferred_element_type=jnp.float32)
        projected += jnp.dot(sib, sib_precond[k], preferred_element_type=jnp.float32)
        out[:, k : k + 1] = jnp.sum(projected * wide, axis=1, keepdims=True)


def score(blocks, acts, own_precond, sib_precond):
    out = pl.pallas_call(
        score_kernel,
        out_shape=jax.ShapeDtypeStruct((GROUP * SEQLEN, QUERIES), jnp.float32),
        in_specs=[VMEM] * (len(blocks) + 6),
        out_specs=VMEM,
        compiler_params=params(20),
        cost_estimate=pl.CostEstimate(
            flops=2 * 512 * 1728 * 1280, bytes_accessed=8 * 1024 * 1024, transcendentals=0
        ),
        name="score",
    )(*blocks, *acts, own_precond, sib_precond)
    return out.reshape(2, 4, GROUP, ROWS, QUERIES)


def act_kernel(order, acts, *refs):
    bases, (kept, other) = refs[:8], refs[8:]
    total = jnp.zeros((acts.shape[1], kept.shape[1]), jnp.float32)
    for m in range(8):
        total += jnp.dot(acts[order[m]], bases[m][...], preferred_element_type=jnp.float32)
    half = acts.shape[1] // 2
    kept[...] = total[:half]
    other[...] = total[half:]


def rotate_acts(order, acts, bases):
    part = jax.ShapeDtypeStruct((acts.shape[1] // 2, bases[0].shape[1]), jnp.float32)
    return pl.pallas_call(
        act_kernel,
        out_shape=(part, part),
        in_specs=[SMEM] + [VMEM] * 9,
        out_specs=(VMEM, VMEM),
        compiler_params=params(9),
        cost_estimate=pl.CostEstimate(
            flops=2 * 288 * 2560 * 640, bytes_accessed=6 * 1024 * 1024, transcendentals=0
        ),
        name="rotate_acts",
    )(order, acts, *bases)


def pad_to(x, *shape, value=0):
    return jnp.pad(x, [(0, n - m) for m, n in zip(x.shape, shape)], constant_values=value)


def per_device(
    train_acts, train_grads, query_acts, query_grads, in_basis, out_basis, eigvals, lengths
):
    x_hi = lax.axis_index("x_hi")
    y = lax.axis_index("y")
    core = lax.axis_index("core")
    x_lo = lax.axis_index("x_lo")
    z = lax.axis_index("z")

    half = in_basis.shape[0]
    count = train_acts.shape[0]
    def own_half(x, flip):
        low = (core == 0) != flip
        return jnp.where(low, x[:, :half], x[:, half:])

    sib_acts = take(own_half(train_acts, True), "core", 1)
    chip_acts = jnp.concatenate(
        [
            own_half(train_acts, False),
            own_half(both_cores(query_acts)[0], False),
            sib_acts,
            own_half(both_cores(query_acts)[1], False),
        ],
        axis=0,
    )
    sync = lax.optimization_barrier
    rows_in, rows_out = out_basis.shape
    deep = -(-rows_in // LANES) * LANES
    wide = -(-rows_out // LANES) * LANES
    own_basis = pad_to(out_basis, deep, wide)
    grad_rows = jnp.concatenate(
        [own_rows_first(train_grads, x_lo, z), both_cores(query_grads)[0]], axis=0
    )
    g = {(0, 0): pad_to(grad_rows, grad_rows.shape[0], deep)}
    g[1, 0] = take(g[0, 0], "x_hi", 1)
    g[0, 1] = take(g[0, 0], "y", 1)
    g[0, 3] = take(g[0, 0], "y", -1)
    sib_basis = take(own_basis, "core", 1)
    acts_z = [take(chip_acts, "z", d) for d in (1, 2, 3)]
    g[1, 0], g[0, 1], g[0, 3], sib_basis, acts_z = sync(
        (g[1, 0], g[0, 1], g[0, 3], sib_basis, acts_z)
    )
    chips = [(h, d) for h in range(2) for d in range(4)]
    groups = (((0, 0), (1, 0), (0, 1), (0, 3)), ((1, 1), (1, 3), (0, 2), (1, 2)))

    g[1, 1] = take(g[1, 0], "y", 1)
    g[1, 3] = take(g[1, 0], "y", -1)
    near_1, up_1, down_1, far_own, far_sib, query_1 = rotate(
        [g[c] for c in groups[0]], own_basis, sib_basis
    )

    far_own, far_sib = take(far_own, "z", -1), take(far_sib, "z", 1)
    g[0, 2] = take(g[0, 1], "y", 1)
    g[1, 2] = take(g[1, 3], "y", -1)
    acts_near = jnp.stack([chip_acts] + acts_z)
    acts_far = take(acts_near, "x_lo", 1)
    far_own, far_sib, g[0, 2], g[1, 2] = sync((far_own, far_sib, g[0, 2], g[1, 2]))

    up_1 = take(up_1.at[0].add(far_own), "z", -1)
    down_1 = take(down_1.at[1].add(far_sib), "z", 1)
    v = {(0, 0): sync((in_basis, g[1, 2]))[0]}
    v[1, 0] = take(v[0, 0], "x_hi", 1)
    v[0, 1] = take(v[0, 0], "y", 1)
    v[0, 3] = take(v[0, 0], "y", -1)
    near_2, up_2, down_2, far_own, far_sib, query_2 = rotate(
        [g[c] for c in groups[1]], own_basis, sib_basis
    )
    far_own, far_sib = take(far_own, "z", -1), take(far_sib, "z", 1)
    query_parts = {c: query_1[s] for s, c in enumerate(groups[0])}
    query_parts.update((c, query_2[s]) for s, c in enumerate(groups[1]))
    query_partial = jnp.concatenate([query_parts[c] for c in chips], axis=0)
    pieces = own_rows_first(query_partial, x_lo, z).reshape(4, 2, ROWS, -1)
    query_z = [take(pieces[d], "z", -d) for d in (1, 2, 3)]
    (up_1, down_1, v[1, 0], v[0, 1], v[0, 3], near_2, up_2, down_2, far_own, far_sib, query_z, acts_far) = sync(
        (up_1, down_1, v[1, 0], v[0, 1], v[0, 3], near_2, up_2, down_2, far_own, far_sib, query_z, acts_far)
    )

    up_2 = take(up_2.at[0].add(far_own), "z", -1)
    down_2 = take(down_2.at[1].add(far_sib), "z", 1)
    kept_1, other_1 = sum_z(near_1, up_1, down_1)
    other_1 = take(other_1, "x_lo", 1)
    v[1, 1] = take(v[1, 0], "y", 1)
    v[1, 3] = take(v[1, 0], "y", -1)
    v[0, 2] = take(v[0, 1], "y", 1)
    v[1, 2] = take(v[1, 3], "y", -1)
    pieces = pieces[0] + query_z[0] + query_z[1] + query_z[2]
    query_x = take(pieces[1], "x_lo", 1)
    acts = jnp.concatenate([acts_near, acts_far], axis=0)
    (up_2, down_2, kept_1, other_1, v[1, 1], v[1, 3], v[0, 2], v[1, 2], query_x, acts) = sync(
        (up_2, down_2, kept_1, other_1, v[1, 1], v[1, 3], v[0, 2], v[1, 2], query_x, acts)
    )

    mean_1 = (kept_1 + other_1).astype(jnp.bfloat16)
    kept_2, other_2 = sum_z(near_2, up_2, down_2)
    other_2 = take(other_2, "x_lo", 1)
    near_1 = [take(mean_1, "z", d) for d in (1, 2, 3)]
    order = jnp.stack([(x_lo ^ x_hi ^ h) * 4 + (y - z + d) % 4 for h, d in chips])
    kept, other = rotate_acts(order.astype(jnp.int32), acts, [v[c] for c in chips])
    rot_acts = (kept + take(other, "core", 1)).astype(jnp.bfloat16)
    rot_acts = jnp.concatenate(
        [own_rows_first(rot_acts[:count], x_lo, z), rot_acts[count:]], axis=0
    )
    pair = jnp.stack([rot_acts, take(rot_acts, "x_hi", 1)])
    query_own = (pieces[0] + query_x).astype(jnp.bfloat16)
    query_near = [take(query_own, "z", d) for d in (1, 2, 3)]

    mean_2 = (kept_2 + other_2).astype(jnp.bfloat16)
    pair_2 = take(mean_2, "x_lo", 1)
    query_near = jnp.stack([query_own] + query_near)
    query_far = take(query_near, "x_lo", 1)
    pairs = [pair, take(pair, "y", 1), take(pair, "y", 2), take(pair, "y", -1)]
    near_1 = [mean_1] + near_1
    near_1_all = jnp.stack(near_1)
    pair_2, query_far, pairs, near_1_all = sync(
        (pair_2, query_far, pairs, near_1_all)
    )

    far_1 = take(near_1_all, "x_lo", 1)
    pair_2 = jnp.stack([mean_2, pair_2])
    pairs_2 = [pair_2] + [take(pair_2, "z", d) for d in (1, 2, 3)]
    query_acts_all = jnp.concatenate([pairs[d][h, count:] for h, d in chips], axis=0)
    query_acts_all = own_rows_first(query_acts_all, x_lo, z).reshape(4, 2, ROWS, -1)
    query_len = 4 * ROWS
    divisor = query_len * (pad_to(eigvals, wide, eigvals.shape[1], value=1.0) + damping)
    precond = []
    for dx, part in enumerate((query_near, query_far)):
        numerator = jnp.dot(
            part.reshape(query_len, -1).T,
            query_acts_all[:, dx].reshape(query_len, -1),
            preferred_element_type=jnp.float32,
        )
        precond.append((numerator / divisor).astype(jnp.bfloat16))
    own_precond = jnp.stack(precond)
    sib_precond = take(own_precond, "core", 1)

    scores = {}
    result = score([near_1_all, far_1], pairs, own_precond, sib_precond)
    pairs_2, result = sync((pairs_2, result))
    for group, part in zip(groups, (result, score(pairs_2, pairs, own_precond, sib_precond))):
        scores.update((c, part[:, :, s]) for s, c in enumerate(group))
    stacked = jnp.stack([scores[c] for c in chips]).reshape(2, 4, 2, 4, ROWS, QUERIES)
    stacked = stacked.transpose(5, 0, 1, 2, 3, 4)
    stacked = jnp.where(x_lo != x_hi, stacked[::-1], stacked)
    stacked = jnp.where(x_hi == 1, stacked[:, ::-1], stacked)
    stacked = jnp.where(x_lo == 1, stacked[:, :, :, ::-1], stacked)
    stacked = turn(turn(stacked, 2, (-y) % 4), 4, (-z) % 4)
    by_sequence = stacked.reshape(QUERIES, 8, SEQLEN).transpose(1, 0, 2)
    by_core = jnp.stack([jnp.where(core == c, by_sequence, 0.0) for c in range(2)], axis=1)
    spread = jnp.broadcast_to(by_core[:, :, None], (8, 2, 8, QUERIES, SEQLEN))
    received = lax.all_to_all(spread.reshape(128, QUERIES, SEQLEN), AXES, 0, 0, tiled=True)
    raw = jnp.sum(received, axis=0)
    valid = (jnp.arange(SEQLEN, dtype=jnp.int32) < lengths[0]).astype(jnp.float32)
    masked = raw * valid[None, :]
    seq_scores = jnp.sum(masked, axis=1, keepdims=True)
    token_scores = lax.dynamic_slice_in_dim(masked, (x_lo * 4 + z) * ROWS, ROWS, axis=1)
    return (token_scores, seq_scores)


def solution(mesh):
    grid = jax.sharding.Mesh(mesh.devices.reshape(SIZES), AXES)
    dp = AXES[:3]
    return jax.shard_map(
        per_device,
        mesh=grid,
        in_specs=(
            P(dp, TENSOR),
            P(dp, TENSOR),
            P(dp, TENSOR),
            P(dp, TENSOR),
            P(dp, TENSOR),
            P(TENSOR, dp),
            P(dp, TENSOR),
            P(dp),
        ),
        out_specs=(P(None, dp + TENSOR), P(None, dp)),
        check_vma=False,
    )
```
